128 devices in a mesh: node: 16 (over y, z), local: 8 (over x, core).
Axes of the slice: x: 4, y: 4, z: 4, core: 2. Of those that a mesh axis runs over, the one named last changes fastest.
Arguments:
- tokens: bfloat16 [8192, 3584], P(('node', 'local')), may hold values from -6 to 6
- norm_gain: float32 [3584], replicated, may hold values from 0.1 to 1.9
- w_gate: bfloat16 [128, 3584, 1024], P(('node', 'local')), may hold values from -0.09375 to 0.09375
- w_up: bfloat16 [128, 3584, 1024], P(('node', 'local')), may hold values from -0.09375 to 0.09375
- w_down: bfloat16 [128, 1024, 3584], P(('node', 'local')), may hold values from -0.1875 to 0.1875
- expert_ids: int32 [8192, 8], P(('node', 'local')), may hold values from 0 to 127, as said below
- gate_weights: float32 [8192, 8], P(('node', 'local')), may hold values from 0.1 to 0.5
- capacity: int32 [128], replicated, may hold values from 2 to 4, as said below
Outputs:
- mixed: bfloat16 [8192, 3584], P(('node', 'local'))
The draws below stay inside these ranges and needn't reach their ends.
Inputs may be any that keep to these rules, and one draw needn't show every extreme that they name: `expert_ids`: each row names 8 distinct experts, all within at most 4 node groups; expert e lies in node group e // 8. In every draw one expert with capacity 4 is named by at least 4 tokens of every micro-batch group. Some expert has capacity exactly 4.
All inputs are finite; a program needn't handle non-finite values.
Results may differ from the reference program's by a relative error of at most 0.0047.
Values may be sent and summed in bfloat16 or wider, within the bound.
A program may use at most 128 MiB of HBM per device.

```python
import jax
import jax.numpy as jnp
from jax import lax

D = 3584
FF = 1024
TOPK = 8
LIMIT = 4
TOK_MB = 32
C = 4
GROUPS = 16
MEMBERS = 8
SPECIALIST_COUNT = 128
WORDPIECE_SUM = 8192


def hot_expert(key):
    return jax.random.randint(jax.random.fold_in(key, 97), (), 0, SPECIALIST_COUNT)


def draw_expert_ids(key, part):
    hot = hot_expert(key)
    key = jax.random.fold_in(key, 1)
    machine_seed, uplift_seed, selection_seed = jax.random.split(key, 3)
    position = jnp.arange(WORDPIECE_SUM)
    forced = position % TOK_MB % (TOK_MB // C) == 0
    node_label = jnp.arange(GROUPS)
    node_score = jax.random.randint(machine_seed, (WORDPIECE_SUM, GROUPS), 0, 4096)
    node_score = node_score + jnp.where(forced[:, None] & (node_label == hot // MEMBERS)[None, :], 4096, 0)
    node_score = node_score * GROUPS + node_label
    _, chosen = lax.top_k(node_score, LIMIT)
    node_ok = jnp.any(chosen[:, :, None] == node_label, axis=1)
    expert_label = jnp.arange(SPECIALIST_COUNT)
    expert_ok = node_ok[:, expert_label // MEMBERS]
    logit_uplift = jax.random.randint(uplift_seed, (SPECIALIST_COUNT,), 0, 4096)
    gating_logit = jax.random.randint(selection_seed, (WORDPIECE_SUM, SPECIALIST_COUNT), 0, 4096) + logit_uplift[None, :]
    gating_logit = gating_logit + jnp.where(forced[:, None] & (expert_label == hot)[None, :], 8192, 0)
    gating_logit = jnp.where(expert_ok, gating_logit * SPECIALIST_COUNT + expert_label, -1 - expert_label)
    _, picked = lax.top_k(gating_logit, TOPK)
    return picked.astype(jnp.int32)


def draw_capacity(key, part):
    hot = hot_expert(key)
    key = jax.random.fold_in(key, 2)
    limits = jax.random.randint(key, (SPECIALIST_COUNT,), 2, C + 1)
    return jnp.where(jnp.arange(SPECIALIST_COUNT) == hot, C, limits).astype(jnp.int32)


def block_scale(stream_key, dims, pieces, least, high):
    gain, own = 1.0, jax.random.fold_in(stream_key, 6)
    for dim, parts in pieces:
        steps = jnp.exp(jax.random.uniform(jax.random.fold_in(own, dim), (parts,), jnp.float32, least / len(pieces), high / len(pieces)))
        gain = gain * jnp.repeat(steps, dims[dim] // parts).reshape([-1 if axis == dim else 1 for axis in range(len(dims))])
    return gain


def centred(rng, shape, width, bound, shards=(), held_as=jnp.bfloat16):
    factor_of = block_scale(rng, shape, shards, -0.22, 0.18) if shards else 1.0
    values = jax.random.normal(rng, shape, jnp.float32) * width * factor_of
    return jnp.minimum(jnp.maximum(values, -bound), bound).astype(held_as)


def setup_inputs(seed: int = 0) -> dict:
    seeds = jax.random.split(jax.random.key(seed), 9)
    tokens = centred(seeds[0], (WORDPIECE_SUM, D), 1.0, 6.0, ((0, 128),))
    norm_gain = jnp.clip(1.0 + 0.18 * jax.random.normal(seeds[1], (D,), jnp.float32), 0.1, 1.9)
    w_gate = centred(seeds[2], (SPECIALIST_COUNT, D, FF), D ** -0.5, 0.09375, ((0, 128),))
    w_up = centred(seeds[3], (SPECIALIST_COUNT, D, FF), D ** -0.5, 0.09375, ((0, 128),))
    w_down = centred(seeds[4], (SPECIALIST_COUNT, FF, D), FF ** -0.5, 0.1875, ((0, 128),))
    expert_ids = draw_expert_ids(jax.random.fold_in(seeds[8], 71), 0)
    gate_weights = jnp.clip(0.1 + 0.4 * jax.random.uniform(seeds[6], (WORDPIECE_SUM, TOPK), jnp.float32) ** block_scale(seeds[6], (WORDPIECE_SUM, TOPK), ((0, 128),), -0.2, 0.2), 0.1, 0.5)
    capacity = draw_capacity(jax.random.fold_in(seeds[8], 71), 0)
    return {"tokens": tokens, "norm_gain": norm_gain, "w_gate": w_gate, "w_up": w_up, "w_down": w_down, "expert_ids": expert_ids, "gate_weights": gate_weights, "capacity": capacity}


def reference(tokens, norm_gain, w_gate, w_up, w_down, expert_ids, gate_weights, capacity):
    residual = tokens.astype(jnp.float32)
    normed = (residual * lax.rsqrt(lax.optimization_barrier(jnp.mean(residual * residual, axis=-1, keepdims=True)) + 1e-06) * norm_gain).astype(jnp.bfloat16)
    group_count = WORDPIECE_SUM // TOK_MB
    labels = jnp.arange(SPECIALIST_COUNT, dtype=jnp.int32)
    onehot = lax.optimization_barrier(jnp.sum((expert_ids[:, :, None] == labels).astype(jnp.int32), axis=1))
    onehot = onehot.reshape(group_count, TOK_MB, SPECIALIST_COUNT)
    before = (jnp.cumsum(onehot, axis=1) - onehot).reshape(WORDPIECE_SUM, SPECIALIST_COUNT)
    order_rank = jnp.take_along_axis(before, expert_ids, axis=1)
    is_kept = order_rank < capacity[expert_ids]
    source_group = (jnp.arange(WORDPIECE_SUM, dtype=jnp.int32) // TOK_MB)[:, None]
    position = jnp.where(is_kept, source_group * C + order_rank, group_count * C).astype(jnp.int32)
    token_index = jnp.broadcast_to(jnp.arange(WORDPIECE_SUM, dtype=jnp.int32)[:, None], expert_ids.shape)
    slot_token = jnp.zeros((SPECIALIST_COUNT, group_count * C), jnp.int32).at[expert_ids, position].set(token_index, mode='drop')
    slot_weight = jnp.zeros((SPECIALIST_COUNT, group_count * C), jnp.float32).at[expert_ids, position].set(gate_weights, mode='drop')

    def one_expert(total, inputs):
        gate_matrix, up_matrix, down_matrix, row_tokens, row_weights = inputs
        batch_rows = normed[row_tokens]
        gate_part = jnp.dot(batch_rows, gate_matrix, preferred_element_type=jnp.float32)
        up_part = jnp.dot(batch_rows, up_matrix, preferred_element_type=jnp.float32)
        hidden = (jax.nn.silu(gate_part) * up_part).astype(jnp.bfloat16)
        answer = jnp.dot(hidden, down_matrix, preferred_element_type=jnp.float32).astype(jnp.bfloat16)
        total = total.at[row_tokens].add(row_weights[:, None] * answer.astype(jnp.float32))
        return (total, None)
    total, _ = lax.scan(one_expert, jnp.zeros((WORDPIECE_SUM, D), jnp.float32), (w_gate, w_up, w_down, slot_token, slot_weight))
    return (residual + total).astype(jnp.bfloat16)
```

```python
import functools

import jax
import jax.numpy as jnp
from jax import lax
from jax.experimental import pallas as pl
from jax.experimental.pallas import tpu as pltpu
from jax.sharding import PartitionSpec as P

MESH = pl.DeviceIdType.MESH
F32, BF16 = jnp.float32, jnp.bfloat16

D = 3584
FF = 1024
HALF = D // 2
W = (640, 640, 512)
OFF = (0, 640, 1280)


def device(x, y, z, c):
    return (y * 4 + z, x * 2 + c)


def expert(x, y, z):
    return (y * 4 + z) * 8 + x * 2


def kernel(
    tok_ref, gain_ref, wg_hbm, wu_hbm, wd_hbm, ids_ref, gates_ref, cap_ref, out_ref,
    wg, wu, wd, normed, tokh, metan, meta, pt, gt, tgx, tgy, tgz,
    stx, sty, stz, rows, hid, retx, rety, retz, cmx, cmy, cmz,
    ptx, pty, ptz, rsx, rsy, rsz, tot, sib,
    wsem, sibs, sibr, s1s, s1r, mts, mtr, dsem, xsem, bsem, rsem, ps, pr,
):
    node, local = lax.axis_index("node"), lax.axis_index("local")
    x, y, z, c = local // 2, node // 4, node % 4, local % 2
    sign = 1 - 2 * c
    tg, st, ret, cm, part, rs = (
        (tgx, tgy, tgz), (stx, sty, stz), (retx, rety, retz), (cmx, cmy, cmz), (ptx, pty, ptz), (rsx, rsy, rsz)
    )

    def remote(src, dst, send, recv, to):
        return pltpu.make_async_remote_copy(
            src_ref=src, dst_ref=dst, send_sem=send, recv_sem=recv, device_id=to, device_id_type=MESH
        )

    def await_bytes(ref, sem):
        pltpu.make_async_copy(ref, ref, sem).wait()

    weights = [
        pltpu.make_async_copy(w_hbm.at[0], w_vmem, wsem.at[i])
        for i, (w_hbm, w_vmem) in enumerate(((wg_hbm, wg), (wu_hbm, wu), (wd_hbm, wd)))
    ]

    barrier = pltpu.get_barrier_semaphore()
    partners = 0
    for dx in range(4):
        for dy in range(4):
            for dz in range(4):
                if dx and dy and dz:
                    continue
                for k in range(2):
                    if dx == dy == dz == 0 and k == 0:
                        continue
                    partners += 1
                    pl.semaphore_signal(
                        barrier, inc=1, device_id_type=MESH,
                        device_id=device((x + dx) % 4, (y + dy) % 4, (z + dz) % 4, (c + k) % 2),
                    )

    resid = tok_ref[...].astype(F32)
    scale = lax.rsqrt(jnp.mean(resid * resid, axis=-1, keepdims=True) + 1e-06)
    normed[...] = (resid * scale * gain_ref[...]).astype(BF16)
    for copy in weights:
        copy.start()

    lane = lax.broadcasted_iota(jnp.int32, (64, 128), 1)
    row = lax.broadcasted_iota(jnp.int32, (64, 128), 0)
    hits = [ids_ref[:, k : k + 1] == lane for k in range(8)]
    named = functools.reduce(jnp.logical_or, hits)
    col64 = lax.broadcasted_iota(jnp.int32, (64, 64), 1)
    row64 = lax.broadcasted_iota(jnp.int32, (64, 64), 0)
    earlier = jnp.logical_and(col64 < row64, col64 // 32 == row64 // 32)
    before = jnp.dot(
        earlier.astype(F32).astype(BF16), named.astype(F32).astype(BF16), preferred_element_type=F32
    )
    group = (row // 32 + c * 2).astype(F32)
    place = jnp.where(before < cap_ref[...].astype(F32), group * 4.0 + before, -1.0)
    info = jnp.zeros((64, 128), F32)
    for k in range(8):
        mine = jnp.sum(jnp.where(hits[k], place, 0.0), axis=1, keepdims=True)
        info = jnp.where(lane == k, ids_ref[:, k : k + 1].astype(F32), info)
        info = jnp.where(lane == 8 + k, mine, info)
        info = jnp.where(lane == 16 + k, gates_ref[:, k : k + 1], info)
    own_rows = pl.ds(pl.multiple_of(c * 64, 64), 64)
    other_rows = pl.ds(pl.multiple_of((1 - c) * 64, 64), 64)
    own_cols = pl.ds(pl.multiple_of(c * HALF, 128), HALF)
    other_cols = pl.ds(pl.multiple_of((1 - c) * HALF, 128), HALF)
    metan[own_rows, :] = info
    tokh[own_rows, :] = normed[:, own_cols]

    pl.semaphore_wait(barrier, partners)

    sibling = device(x, y, z, 1 - c)
    swap = (
        remote(normed.at[:, other_cols], tokh.at[own_rows], sibs.at[0], sibr.at[0], sibling),
        remote(metan.at[own_rows], metan.at[own_rows], sibs.at[1], sibr.at[1], sibling),
    )
    for copy in swap:
        copy.start()
    for copy in swap:
        copy.wait()
    meta[0] = jnp.transpose(metan[...])[0:24, :]

    def along(p, d):
        return (x + d * (p == 0)) % 4, (y + d * (p == 1)) % 4, (z + d * (p == 2)) % 4

    firsts = []
    for d in (1, 3, 2):
        for p in range(3):
            to = device(*along(p, d), c)
            n = 3 * p + d - 1
            firsts.append(remote(meta.at[0], meta.at[1 + n], mts.at[n], mtr.at[n], to))
            firsts.append(
                remote(tokh.at[:, pl.ds(OFF[p], W[p])], tg[p].at[d - 1], s1s.at[n], s1r.at[n], to)
            )
    for copy in firsts:
        copy.start()

    ids128 = lax.broadcasted_iota(jnp.int32, (128, 128), 0).astype(F32)

    def tables(n):
        at = jnp.full((128, 128), -1.0, F32)
        weight = jnp.zeros((128, 128), F32)
        for k in range(8):
            hit = meta[n, k : k + 1, :] == ids128
            at = jnp.where(hit, meta[n, 8 + k : 9 + k, :], at)
            weight = jnp.where(hit, meta[n, 16 + k : 17 + k, :], weight)
        pt[n] = at
        gt[n] = weight

    tables(0)
    for copy in firsts:
        copy.wait_recv()

    def more_tables(n, carry):
        tables(n)
        return carry

    lax.fori_loop(1, 10, more_tables, 0)

    slot = lax.broadcasted_iota(jnp.int32, (16, 128), 0).astype(F32)

    def chips(p, q, i):
        if p == 0:
            return x, (y + i // 4) % 4, (z + i % 4) % 4
        if p == 1:
            return (x + 2 * (i // 4) + q) % 4, y, (z + i % 4) % 4
        return (x + 2 * (i // 4) + q) % 4, (y + i % 4) % 4, z

    def table_of(p, d):
        return jnp.where(d == 0, 0, 3 * p + d)

    def picks(p, q, n, base, weighted):
        blocks = []
        for i in range(8):
            e = expert(*chips(p, q, base + i))
            for k in range(2):
                hit = pt[n, pl.ds(e + k, 1), :] == slot
                value = gt[n, pl.ds(e + k, 1), :] if weighted else 1.0
                blocks.append(jnp.where(hit, value, 0.0))
        return jnp.concatenate(blocks, axis=0)

    def stage(q):
        for p in (1, 2):
            for d in range(4):
                source = tokh[:, OFF[p] : OFF[p] + W[p]] if d == 0 else tg[p][d - 1]
                chosen = picks(p, q, 0 if d == 0 else 3 * p + d, 0, False).astype(BF16)
                block = jnp.dot(chosen, source, preferred_element_type=F32).astype(BF16)
                st[p][d, q] = block.reshape(16, 16, W[p])
        for h in range(2):
            d = 2 * h + q
            source = tokh[:, OFF[0] : OFF[0] + W[0]] if d == 0 else tg[0][d - 1]
            for base in (0, 8):
                chosen = picks(0, q, 0 if d == 0 else d, base, False).astype(BF16)
                block = jnp.dot(chosen, source, preferred_element_type=F32).astype(BF16)
                st[0][q, h, base * 2 : base * 2 + 16] = block.reshape(16, 16, W[0])

    def columns(half, p):
        return pl.ds(pl.multiple_of(half * HALF + OFF[p], 128), W[p])

    def exchange(q, back):
        def one(src, dst, sems, cls, to, here):
            @pl.when(here)
            def _():
                pltpu.make_async_copy(src, dst, sems.at[cls, q] if back else sems.at[q]).start()

            @pl.when(jnp.logical_not(here))
            def _():
                remote(
                    src, dst, (bsem if back else dsem).at[cls, q], sems.at[cls, q] if back else sems.at[q], to
                ).start()

        def step(i, carry):
            h, b, k = i // 8, (sign * ((i // 2) % 4) + 4) % 4, i % 2
            if q == 1:
                h = h * sign + c
            dx = 2 * h + q
            i2 = h * 8 + b * 2 + k
            u, v = (sign * (i // 4) + 4) % 4, (sign * (i % 4) + 4) % 4
            if not back:
                one(sty.at[:, q, i2], rows.at[q, h, :, b, :, columns(c, 1)], xsem, 1,
                    device((x + dx) % 4, y, (z + b) % 4, k), jnp.logical_and(dx + b == 0, k == c))
                one(stz.at[:, q, i2], rows.at[q, h, b, :, :, columns(c, 2)], xsem, 2,
                    device((x + dx) % 4, (y + b) % 4, z, k), jnp.logical_and(dx + b == 0, k == c))
                for m in range(2):
                    one(stx.at[q, :, u * 8 + v * 2 + m], rows.at[q, :, u, v, :, columns(c, 0)], xsem, 0,
                        device(x, (y + u) % 4, (z + v) % 4, m), jnp.logical_and(u + v == 0, m == c))
            else:
                one(rows.at[q, h, :, b, :, columns(k, 1)], rety.at[:, q, h * 8 + b * 2 + c], rsem, 1,
                    device((x - dx + 4) % 4, y, (z - b + 4) % 4, k), jnp.logical_and(dx + b == 0, k == c))
                one(rows.at[q, h, b, :, :, columns(k, 2)], retz.at[:, q, h * 8 + b * 2 + c], rsem, 2,
                    device((x - dx + 4) % 4, (y - b + 4) % 4, z, k), jnp.logical_and(dx + b == 0, k == c))
                for m in range(2):
                    one(rows.at[q, :, u, v, :, columns(m, 0)], retx.at[q, :, u * 8 + v * 2 + c], rsem, 0,
                        device(x, (y - u + 4) % 4, (z - v + 4) % 4, m), jnp.logical_and(u + v == 0, m == c))
            return carry

        lax.fori_loop(0, 16, step, 0)

    for q in range(2):
        stage(q)
        exchange(q, False)

    for p in (1, 2):
        for d in range(4):
            for q in range(2):
                block = picks(p, q, 0 if d == 0 else 3 * p + d, 0, True)
                cm[p][d, :, q * 256 : q * 256 + 256] = jnp.transpose(block).astype(BF16)
    for q in range(2):
        for h in range(2):
            d = 2 * h + q
            for base in (0, 8):
                block = picks(0, q, d, base, True)
                cm[0][d, :, base * 32 : base * 32 + 256] = jnp.transpose(block).astype(BF16)

    for copy in weights:
        copy.wait()
    for q in range(2):
        await_bytes(rows.at[q], xsem.at[q])

        def up(n, carry):
            cols = pl.ds(pl.multiple_of(n * 256, 256), 256)
            batch = rows[q].reshape(512, D)
            gate = jnp.dot(batch, wg[:, cols], preferred_element_type=F32)
            lift = jnp.dot(batch, wu[:, cols], preferred_element_type=F32)
            hid[:, cols] = (gate / (1.0 + jnp.exp(-gate)) * lift).astype(BF16)
            return carry

        lax.fori_loop(0, FF // 256, up, 0)

        def down(n, carry):
            cols = pl.ds(pl.multiple_of(n * 512, 512), 512)
            answer = jnp.dot(hid[...], wd[:, cols], preferred_element_type=F32).astype(BF16)
            rows[q, :, :, :, :, cols] = answer.reshape(2, 4, 4, 16, 512)
            return carry

        lax.fori_loop(0, D // 512, down, 0)
        exchange(q, True)

    lasts = []

    def reduce(p, d, answers):
        total = jnp.dot(cm[p][d], answers, preferred_element_type=F32)
        if d == 0:
            tot[:, OFF[p] : OFF[p] + W[p]] = total
        else:
            part[p][d - 1] = total.astype(BF16)
            n = 3 * p + d - 1
            to = device(*along(p, 4 - d), c)
            copy = remote(part[p].at[d - 1], rs[p].at[d - 1], ps.at[n], pr.at[n], to)
            copy.start()
            lasts.append((p, d, copy))

    for q in range(2):
        await_bytes(retx.at[q], rsem.at[0, q])
        for h in range(2):
            reduce(0, 2 * h + q, retx[q, h].reshape(512, W[0]))
    for p in (1, 2):
        for q in range(2):
            await_bytes(ret[p].at[:, q], rsem.at[p, q])
        for d in range(4):
            reduce(p, d, ret[p][d].reshape(512, W[p]))
    for p, d, copy in lasts:
        copy.wait_recv()
    for p in range(3):
        cols = slice(OFF[p], OFF[p] + W[p])
        tot[:, cols] = tot[:, cols] + (
            rs[p][0].astype(F32) + rs[p][1].astype(F32) + rs[p][2].astype(F32)
        )
    last = remote(tot.at[other_rows], sib, sibs.at[2], sibr.at[2], sibling)
    last.start()
    out_ref[:, own_cols] = (tok_ref[:, own_cols].astype(F32) + tot[own_rows, :]).astype(BF16)
    last.wait_recv()
    out_ref[:, other_cols] = (tok_ref[:, other_cols].astype(F32) + sib[...]).astype(BF16)

    last.wait_send()
    for copy in firsts:
        copy.wait_send()
    for p, d, copy in lasts:
        copy.wait_send()
    for sems, boxes in ((dsem, st), (bsem, ret)):
        for q in range(2):
            await_bytes(boxes[0].at[q, :, pl.ds(0, 31)], sems.at[0, q])
            for p in (1, 2):
                await_bytes(boxes[p].at[:, q, pl.ds(0, 15 + q)], sems.at[p, q])


def shards(tokens, norm_gain, w_gate, w_up, w_down, expert_ids, gate_weights, capacity):
    vmem, dma = pltpu.VMEM, pltpu.SemaphoreType.DMA
    whole = pl.BlockSpec(memory_space=pltpu.VMEM)
    hbm = pl.BlockSpec(memory_space=pl.ANY)
    relay = [vmem((2, 2, 32, 16, W[0]), BF16)] + [vmem((4, 2, 16, 16, w), BF16) for w in W[1:]]
    three = [vmem((3, 128, w), BF16) for w in W]
    return pl.pallas_call(
        kernel,
        out_shape=jax.ShapeDtypeStruct(tokens.shape, BF16),
        in_specs=[whole, whole, hbm, hbm, hbm, whole, whole, whole],
        out_specs=whole,
        scratch_shapes=[
            vmem((D, FF), BF16), vmem((D, FF), BF16), vmem((FF, D), BF16),
            vmem((64, D), BF16), vmem((128, HALF), BF16), vmem((128, 128), F32), vmem((10, 24, 128), F32),
            vmem((10, 128, 128), F32), vmem((10, 128, 128), F32),
            *three,
            *relay,
            vmem((2, 2, 4, 4, 16, D), BF16), vmem((512, FF), BF16),
            *relay,
            *[vmem((4, 128, 512), BF16) for _ in range(3)],
            *three,
            *three,
            vmem((128, HALF), F32), vmem((64, HALF), F32),
            dma((3,)), dma((3,)), dma((3,)), dma((9,)), dma((9,)), dma((9,)), dma((9,)),
            dma((3, 2)), dma((2,)), dma((3, 2)), dma((3, 2)), dma((9,)), dma((9,)),
        ],
        compiler_params=pltpu.CompilerParams(
            collective_id=0, has_side_effects=True, vmem_limit_bytes=64 * 2**20
        ),
        cost_estimate=pl.CostEstimate(flops=23 * 10**9, bytes_accessed=23 * 10**6, transcendentals=10**6),
    )(
        tokens, norm_gain.reshape(1, D), w_gate, w_up, w_down, expert_ids, gate_weights,
        capacity.reshape(1, 128),
    )


def solution(mesh):
    both = ("node", "local")
    in_specs = (
        P(both, None), P(), P(both, None, None), P(both, None, None), P(both, None, None),
        P(both, None), P(both, None), P(),
    )
    return jax.shard_map(shards, mesh=mesh, in_specs=in_specs, out_specs=P(both, None), check_vma=False)
```

```python
import functools

import jax
import jax.numpy as jnp
from jax import lax
from jax.experimental import pallas as pl
from jax.experimental.pallas import tpu as pltpu
from jax.sharding import PartitionSpec as P

MESH = pl.DeviceIdType.MESH
F32, BF16 = jnp.float32, jnp.bfloat16

D = 3584
FF = 1024
HALF = D // 2
W = (640, 640, 512)
OFF = (0, 640, 1280)


def device(x, y, z, c):
    return (y * 4 + z, x * 2 + c)


def expert(x, y, z):
    return (y * 4 + z) * 8 + x * 2


def kernel(
    tok_ref, gain_ref, wg_hbm, wu_hbm, wd_hbm, ids_ref, gates_ref, cap_ref, out_ref,
    wg, wu, wd, normed, tokh, own_info, sib_info, meta, pt, gt, tgx, tgy, tgz,
    stx, sty, stz, rows, hid, retx, rety, retz, cmx, cmy, cmz,
    ptx, pty, ptz, rsx, rsy, rsz, tot, sib,
    wsem, sibs, sibr, s1s, s1r, mts, mtr, dsem, xsem, bsem, rsem, ps, pr,
):
    node, local = lax.axis_index("node"), lax.axis_index("local")
    x, y, z, c = local // 2, node // 4, node % 4, local % 2
    sign = 1 - 2 * c
    tg, st, ret, cm, part, rs = (
        (tgx, tgy, tgz), (stx, sty, stz), (retx, rety, retz), (cmx, cmy, cmz), (ptx, pty, ptz), (rsx, rsy, rsz)
    )

    def remote(src, dst, send, recv, to):
        return pltpu.make_async_remote_copy(
            src_ref=src, dst_ref=dst, send_sem=send, recv_sem=recv, device_id=to, device_id_type=MESH
        )

    def await_bytes(ref, sem):
        pltpu.make_async_copy(ref, ref, sem).wait()

    weights = [
        pltpu.make_async_copy(w_hbm.at[0], w_vmem, wsem.at[i])
        for i, (w_hbm, w_vmem) in enumerate(((wg_hbm, wg), (wu_hbm, wu), (wd_hbm, wd)))
    ]

    barrier = pltpu.get_barrier_semaphore()
    partners = 0
    for dx in range(4):
        for dy in range(4):
            for dz in range(4):
                if dx and dy and dz:
                    continue
                for k in range(2):
                    if dx == dy == dz == 0 and k == 0:
                        continue
                    partners += 1
                    pl.semaphore_signal(
                        barrier, inc=1, device_id_type=MESH,
                        device_id=device((x + dx) % 4, (y + dy) % 4, (z + dz) % 4, (c + k) % 2),
                    )

    resid = tok_ref[...].astype(F32)
    scale = lax.rsqrt(jnp.mean(resid * resid, axis=-1, keepdims=True) + 1e-06)
    normed[...] = (resid * scale * gain_ref[...].reshape(1, D)).astype(BF16)
    for copy in weights:
        copy.start()

    twice = lambda a: jnp.concatenate([a, a], axis=1)
    ids = twice(ids_ref[...])
    names = lax.broadcasted_iota(jnp.int32, (128, 128), 0)
    lanes = lax.broadcasted_iota(jnp.int32, (128, 128), 1)
    hits = [ids[k : k + 1, :] == names for k in range(8)]
    named = functools.reduce(jnp.logical_or, hits)
    earlier = jnp.logical_and(names < lanes, names // 32 == lanes // 32)
    before = jnp.dot(
        named.astype(F32).astype(BF16), earlier.astype(F32).astype(BF16), preferred_element_type=F32
    )
    group = (lanes // 32 % 2 + c * 2).astype(F32)
    limit = jnp.transpose(jnp.broadcast_to(cap_ref[...].astype(F32), (128, 128)))
    place = jnp.where(before < limit, group * 4.0 + before, -1.0)
    own_info[0:8, :] = ids.astype(F32)
    for k in range(8):
        own_info[8 + k : 9 + k, :] = jnp.sum(jnp.where(hits[k], place, 0.0), axis=0, keepdims=True)
    own_info[16:24, :] = twice(gates_ref[...])
    own_rows = pl.ds(pl.multiple_of(c * 64, 64), 64)
    other_rows = pl.ds(pl.multiple_of((1 - c) * 64, 64), 64)
    own_cols = pl.ds(pl.multiple_of(c * HALF, 128), HALF)
    other_cols = pl.ds(pl.multiple_of((1 - c) * HALF, 128), HALF)
    tokh[own_rows, :] = normed[:, own_cols]

    pl.semaphore_wait(barrier, partners)

    sibling = device(x, y, z, 1 - c)
    swap = (
        remote(normed.at[:, other_cols], tokh.at[own_rows], sibs.at[0], sibr.at[0], sibling),
        remote(own_info, sib_info, sibs.at[1], sibr.at[1], sibling),
    )
    for copy in swap:
        copy.start()
    for copy in swap:
        copy.wait()
    side = lax.broadcasted_iota(jnp.int32, (24, 128), 1) // 64
    meta[0] = jnp.where(side == c, own_info[...], sib_info[...])

    def along(p, d):
        if p == 0:
            return (x + d) % 4, y, z
        on_z = c if p == 1 else 1 - c
        return x, (y + d * (1 - on_z)) % 4, (z + d * on_z) % 4

    firsts = []
    for d in (1, 3, 2):
        for p in range(3):
            to = device(*along(p, d), c)
            n = 3 * p + d - 1
            firsts.append(remote(meta.at[0], meta.at[1 + n], mts.at[n], mtr.at[n], to))
            firsts.append(
                remote(tokh.at[:, pl.ds(OFF[p], W[p])], tg[p].at[d - 1], s1s.at[n], s1r.at[n], to)
            )
    for copy in firsts:
        copy.start()

    ids128 = lax.broadcasted_iota(jnp.int32, (128, 128), 0).astype(F32)

    def tables(n):
        at = jnp.full((128, 128), -1.0, F32)
        weight = jnp.zeros((128, 128), F32)
        for k in range(8):
            hit = meta[n, k : k + 1, :] == ids128
            at = jnp.where(hit, meta[n, 8 + k : 9 + k, :], at)
            weight = jnp.where(hit, meta[n, 16 + k : 17 + k, :], weight)
        pt[n] = at
        gt[n] = weight

    tables(0)
    slot = lax.broadcasted_iota(jnp.int32, (16, 128), 0).astype(F32)

    def chips(p, q, i):
        if p == 0:
            return x, (y + i // 4) % 4, (z + i % 4) % 4
        on_z = c if p == 1 else 1 - c
        return (x + 2 * (i // 4) + q) % 4, (y + i % 4 * on_z) % 4, (z + i % 4 * (1 - on_z)) % 4

    def picks(p, q, n, base, weighted):
        blocks = []
        for i in range(8):
            e = expert(*chips(p, q, base + i))
            for k in range(2):
                hit = pt[n, pl.ds(e + k, 1), :] == slot
                value = gt[n, pl.ds(e + k, 1), :] if weighted else 1.0
                blocks.append(jnp.where(hit, value, 0.0))
        return jnp.concatenate(blocks, axis=0)

    def stage(q, shifts):
        for p in (1, 2):
            for d in shifts:
                source = tokh[:, OFF[p] : OFF[p] + W[p]] if d == 0 else tg[p][d - 1]
                chosen = picks(p, q, 0 if d == 0 else 3 * p + d, 0, False).astype(BF16)
                block = jnp.dot(chosen, source, preferred_element_type=F32).astype(BF16)
                st[p][d, q] = block.reshape(16, 16, W[p])
        for d in shifts:
            if d % 2 != q:
                continue
            source = tokh[:, OFF[0] : OFF[0] + W[0]] if d == 0 else tg[0][d - 1]
            for base in (0, 8):
                chosen = picks(0, q, d, base, False).astype(BF16)
                block = jnp.dot(chosen, source, preferred_element_type=F32).astype(BF16)
                st[0][q, d // 2, base * 2 : base * 2 + 16] = block.reshape(16, 16, W[0])

    def columns(half, p):
        return pl.ds(pl.multiple_of(half * HALF + OFF[p], 128), W[p])

    def exchange(q, back, shifts):
        first, count = shifts
        near = pl.ds(first, count)
        half = [d // 2 for d in range(first, first + count) if d % 2 == q]
        pair = pl.ds(half[0], len(half)) if half else None
        sends = bsem if back else dsem

        def one(src, dst, p, to, here):
            arrived = rsem.at[p, q + (back and q == 1 and first == 0)] if back else xsem.at[q]

            @pl.when(here)
            def _():
                pltpu.make_async_copy(src, dst, arrived).start()

            @pl.when(jnp.logical_not(here))
            def _():
                remote(src, dst, sends.at[p, q], arrived, to).start()

        def step(i, carry):
            h, b, k = i // 8, (sign * ((i // 2) % 4) + 4) % 4, i % 2
            if q == 1:
                h = h * sign + c
            dx = 2 * h + q
            u, v = (sign * (i // 4) + 4) % 4, (sign * (i % 4) + 4) % 4
            turn = -1 if back else 1
            here = jnp.logical_and(dx + b == 0, k == c)
            relay, box = (k, h * 8 + b * 2 + c) if back else (c, h * 8 + b * 2 + k)

            def move(box_ref, rows_ref, p, to, here):
                one(*((rows_ref, box_ref) if back else (box_ref, rows_ref)), p, to, here)

            if pair is not None:
                for m in range(2):
                    relay0, box0 = (m, u * 8 + v * 2 + c) if back else (c, u * 8 + v * 2 + m)
                    move((retx if back else stx).at[q, pair, box0], rows.at[q, pair, u, v, :, columns(relay0, 0)],
                         0, device(x, (y + turn * u + 4) % 4, (z + turn * v + 4) % 4, m),
                         jnp.logical_and(u + v == 0, m == c))
            for r in range(2):
                @pl.when((k if back else c) == r)
                def _():
                    along_y, along_z = 1 + r, 2 - r
                    move((ret if back else st)[along_y].at[near, q, box],
                         rows.at[q, h, near, b, :, columns(relay, along_y)], along_y,
                         device((x + turn * dx + 4) % 4, y, (z + turn * b + 4) % 4, k), here)
                    move((ret if back else st)[along_z].at[near, q, box],
                         rows.at[q, h, b, near, :, columns(relay, along_z)], along_z,
                         device((x + turn * dx + 4) % 4, (y + turn * b + 4) % 4, z, k), here)
            return carry

        lax.fori_loop(0, 16, step, 0)

    stage(0, (0,))
    exchange(0, False, (0, 1))
    for copy in firsts:
        copy.wait_recv()

    def more_tables(n, carry):
        tables(n)
        return carry

    lax.fori_loop(1, 10, more_tables, 0)
    stage(0, (1, 2, 3))
    exchange(0, False, (1, 3))
    stage(1, (0, 1, 2, 3))
    exchange(1, False, (0, 4))

    for p in (1, 2):
        for d in range(4):
            for q in range(2):
                block = picks(p, q, 0 if d == 0 else 3 * p + d, 0, True)
                cm[p][d, :, q * 256 : q * 256 + 256] = jnp.transpose(block).astype(BF16)
    for q in range(2):
        for h in range(2):
            d = 2 * h + q
            for base in (0, 8):
                block = picks(0, q, d, base, True)
                cm[0][d, :, base * 32 : base * 32 + 256] = jnp.transpose(block).astype(BF16)

    for copy in weights:
        copy.wait()
    for q in range(2):
        await_bytes(rows.at[q], xsem.at[q])

        def up(n, carry):
            cols = pl.ds(pl.multiple_of(n * 256, 256), 256)
            batch = rows[q].reshape(512, D)
            gate = jnp.dot(batch, wg[:, cols], preferred_element_type=F32)
            lift = jnp.dot(batch, wu[:, cols], preferred_element_type=F32)
            hid[:, cols] = (gate / (1.0 + jnp.exp(-gate)) * lift).astype(BF16)
            return carry

        lax.fori_loop(0, FF // 256, up, 0)

        def down(n, carry):
            cols = pl.ds(pl.multiple_of(n * 512, 512), 512)
            answer = jnp.dot(hid[...], wd[:, cols], preferred_element_type=F32).astype(BF16)
            rows[q, :, :, :, :, cols] = answer.reshape(2, 4, 4, 16, 512)
            return carry

        lax.fori_loop(0, D // 512, down, 0)
        if q == 0:
            exchange(0, True, (0, 4))
        else:
            exchange(1, True, (1, 3))
            exchange(1, True, (0, 1))

    lasts = []

    def reduce(p, d, answers):
        total = jnp.dot(cm[p][d], answers, preferred_element_type=F32)
        if d == 0:
            tot[:, OFF[p] : OFF[p] + W[p]] = total
        else:
            part[p][d - 1] = total.astype(BF16)
            n = 3 * p + d - 1
            to = device(*along(p, 4 - d), c)
            copy = remote(part[p].at[d - 1], rs[p].at[d - 1], ps.at[n], pr.at[n], to)
            copy.start()
            lasts.append((p, d, copy))

    for q in range(2):
        await_bytes(retx.at[q], rsem.at[0, q])
        for h in range(2):
            reduce(0, 2 * h + q, retx[q, h].reshape(512, W[0]))
    for p in (1, 2):
        await_bytes(ret[p].at[:, 0], rsem.at[p, 0])
        await_bytes(ret[p].at[pl.ds(1, 3), 1], rsem.at[p, 1])
        for d in range(1, 4):
            reduce(p, d, ret[p][d].reshape(512, W[p]))
    for p in (1, 2):
        await_bytes(ret[p].at[0, 1], rsem.at[p, 2])
        reduce(p, 0, ret[p][0].reshape(512, W[p]))
    for p, d, copy in lasts:
        copy.wait_recv()
    for p in range(3):
        cols = slice(OFF[p], OFF[p] + W[p])
        tot[:, cols] = tot[:, cols] + (
            rs[p][0].astype(F32) + rs[p][1].astype(F32) + rs[p][2].astype(F32)
        )
    last = remote(tot.at[other_rows], sib, sibs.at[2], sibr.at[2], sibling)
    last.start()
    out_ref[:, own_cols] = (tok_ref[:, own_cols].astype(F32) + tot[own_rows, :]).astype(BF16)
    last.wait_recv()
    out_ref[:, other_cols] = (tok_ref[:, other_cols].astype(F32) + sib[...]).astype(BF16)

    last.wait_send()
    for copy in firsts:
        copy.wait_send()
    for p, d, copy in lasts:
        copy.wait_send()
    for sems, boxes in ((dsem, st), (bsem, ret)):
        for q in range(2):
            await_bytes(boxes[0].at[q, :, pl.ds(0, 31)], sems.at[0, q])
            for p in (1, 2):
                await_bytes(boxes[p].at[:, q, pl.ds(0, 15 + q)], sems.at[p, q])


def shards(tokens, norm_gain, w_gate, w_up, w_down, expert_ids, gate_weights, capacity):
    vmem, dma = pltpu.VMEM, pltpu.SemaphoreType.DMA
    whole = pl.BlockSpec(memory_space=pltpu.VMEM)
    hbm = pl.BlockSpec(memory_space=pl.ANY)
    relay = [vmem((2, 2, 32, 16, W[0]), BF16)] + [vmem((4, 2, 16, 16, w), BF16) for w in W[1:]]
    three = [vmem((3, 128, w), BF16) for w in W]
    return pl.pallas_call(
        kernel,
        out_shape=jax.ShapeDtypeStruct(tokens.shape, BF16),
        in_specs=[whole, whole, hbm, hbm, hbm, whole, whole, whole],
        out_specs=whole,
        scratch_shapes=[
            vmem((D, FF), BF16), vmem((D, FF), BF16), vmem((FF, D), BF16),
            vmem((64, D), BF16), vmem((128, HALF), BF16), vmem((24, 128), F32), vmem((24, 128), F32), vmem((10, 24, 128), F32),
            vmem((10, 128, 128), F32), vmem((10, 128, 128), F32),
            *three,
            *relay,
            vmem((2, 2, 4, 4, 16, D), BF16), vmem((512, FF), BF16),
            *relay,
            *[vmem((4, 128, 512), BF16) for _ in range(3)],
            *three,
            *three,
            vmem((128, HALF), F32), vmem((64, HALF), F32),
            dma((3,)), dma((3,)), dma((3,)), dma((9,)), dma((9,)), dma((9,)), dma((9,)),
            dma((3, 2)), dma((2,)), dma((3, 2)), dma((3, 3)), dma((9,)), dma((9,)),
        ],
        compiler_params=pltpu.CompilerParams(
            collective_id=0, has_side_effects=True, vmem_limit_bytes=64 * 2**20
        ),
        cost_estimate=pl.CostEstimate(flops=23 * 10**9, bytes_accessed=23 * 10**6, transcendentals=10**6),
    )(
        tokens, norm_gain, w_gate, w_up, w_down, expert_ids.T, gate_weights.T,
        capacity.reshape(1, 128),
    )


def solution(mesh):
    both = ("node", "local")
    in_specs = (
        P(both, None), P(), P(both, None, None), P(both, None, None), P(both, None, None),
        P(both, None), P(both, None), P(),
    )
    return jax.shard_map(shards, mesh=mesh, in_specs=in_specs, out_specs=P(both, None), check_vma=False)
```

```python
import functools

import jax
import jax.numpy as jnp
from jax import lax
from jax.experimental import pallas as pl
from jax.experimental.pallas import tpu as pltpu
from jax.sharding import PartitionSpec as P

MESH = pl.DeviceIdType.MESH
F32, BF16 = jnp.float32, jnp.bfloat16

D = 3584
FF = 1024
HALF = D // 2
W = (640, 640, 512)
OFF = (0, 640, 1280)
AXES = ((0, 1, 2), (1, 2, 0), (2, 0, 1))
NOW = 4
PLACE = (0, 2, 1, 3)
KINDS = ((0, 0, 0), (1, 2, 8), (2, 3, 16), (1, 1, 24), (2, 1, 28))


def device(x, y, z, c):
    return (y * 4 + z, x * 2 + c)


def expert(x, y, z):
    return (y * 4 + z) * 8 + x * 2


def kernel(
    tok_ref, gain_ref, wg_hbm, wu_hbm, wd_hbm, ids_ref, gates_ref, cap_ref, out_ref,
    wg, wu, wd, normed, tokh, own_info, sib_info, meta, tk0, tk1, tk2,
    st0, st1, st2, rows, hid, ret0, ret1, ret2, line, far,
    rb0, rb1, rb2, rs0, rs1, rs2, tot, sib,
    wsem, sibs, sibr, s1s, s1r, mts, mtr, s2s, s2r, m2s, m2r, dsem, xsem, bsem, rsem, qs, qr, ps, pr,
):
    node, local = lax.axis_index("node"), lax.axis_index("local")
    x, y, z, c = local // 2, node // 4, node % 4, local % 2
    sign = 1 - 2 * c
    tk, st, ret, rb, rs = (tk0, tk1, tk2), (st0, st1, st2), (ret0, ret1, ret2), (rb0, rb1, rb2), (rs0, rs1, rs2)

    def chip(p, da, db, dc):
        place = [x, y, z]
        for axis, d in zip(AXES[p], (da, db, dc)):
            place[axis] = (place[axis] + d + 4) % 4
        return place

    def remote(src, dst, send, recv, to):
        return pltpu.make_async_remote_copy(
            src_ref=src, dst_ref=dst, send_sem=send, recv_sem=recv, device_id=to, device_id_type=MESH
        )

    def await_bytes(ref, sem):
        pltpu.make_async_copy(ref, ref, sem).wait()

    weights = [
        pltpu.make_async_copy(w_hbm.at[0], w_vmem, wsem.at[i])
        for i, (w_hbm, w_vmem) in enumerate(((wg_hbm, wg), (wu_hbm, wu), (wd_hbm, wd)))
    ]

    barrier = pltpu.get_barrier_semaphore()
    partners = 0
    for dx in range(4):
        for dy in range(4):
            for dz in range(4):
                if dx and dy and dz:
                    continue
                for k in range(2):
                    if dx == dy == dz == 0 and k == 0:
                        continue
                    partners += 1
                    pl.semaphore_signal(
                        barrier, inc=1, device_id_type=MESH,
                        device_id=device((x + dx) % 4, (y + dy) % 4, (z + dz) % 4, (c + k) % 2),
                    )

    resid = tok_ref[...].astype(F32)
    scale = lax.rsqrt(jnp.mean(resid * resid, axis=-1, keepdims=True) + 1e-06)
    normed[...] = (resid * scale * gain_ref[...].reshape(1, D)).astype(BF16)
    for copy in weights:
        copy.start()

    twice = lambda a: jnp.concatenate([a, a], axis=1)
    ids = twice(ids_ref[...])
    names = lax.broadcasted_iota(jnp.int32, (128, 128), 0)
    lanes = lax.broadcasted_iota(jnp.int32, (128, 128), 1)
    hits = [ids[k : k + 1, :] == names for k in range(8)]
    named = functools.reduce(jnp.logical_or, hits)
    earlier = jnp.logical_and(names < lanes, names // 32 == lanes // 32)
    before = jnp.dot(
        named.astype(F32).astype(BF16), earlier.astype(F32).astype(BF16), preferred_element_type=F32
    )
    group = (lanes // 32 % 2 + c * 2).astype(F32)
    limit = jnp.transpose(jnp.broadcast_to(cap_ref[...].astype(F32), (128, 128)))
    place = jnp.where(before < limit, group * 4.0 + before, -1.0)
    own_info[0:8, :] = ids.astype(F32)
    for k in range(8):
        own_info[8 + k : 9 + k, :] = jnp.sum(jnp.where(hits[k], place, 0.0), axis=0, keepdims=True)
    own_info[16:24, :] = twice(gates_ref[...])
    own_rows = pl.ds(pl.multiple_of(c * 64, 64), 64)
    other_rows = pl.ds(pl.multiple_of((1 - c) * 64, 64), 64)
    own_cols = pl.ds(pl.multiple_of(c * HALF, 128), HALF)
    other_cols = pl.ds(pl.multiple_of((1 - c) * HALF, 128), HALF)
    tokh[own_rows, :] = normed[:, own_cols]

    pl.semaphore_wait(barrier, partners)

    sibling = device(x, y, z, 1 - c)
    swap = (
        remote(normed.at[:, other_cols], tokh.at[own_rows], sibs.at[0], sibr.at[0], sibling),
        remote(own_info, sib_info, sibs.at[1], sibr.at[1], sibling),
    )
    for copy in swap:
        copy.start()
    for copy in swap:
        copy.wait()
    side = lax.broadcasted_iota(jnp.int32, (24, 128), 1) // 64
    for p in range(3):
        meta[p, 0, 0] = jnp.where(side == c, own_info[...], sib_info[...])
        tk[p][0, 0] = tokh[:, OFF[p] : OFF[p] + W[p]]

    firsts, seconds, thirds = [], [], []
    for d in (1, 3, 2):
        for p in range(3):
            to = device(*chip(p, d, 0, 0), c)
            n = 3 * p + d - 1
            firsts.append(remote(meta.at[p, 0, 0], meta.at[p, 0, PLACE[d]], mts.at[n], mtr.at[n], to))
            firsts.append(remote(tk[p].at[0, 0], tk[p].at[0, PLACE[d]], s1s.at[n], s1r.at[n], to))
    for copies, m, span in ((seconds, 0, pl.ds(0, 1)), (thirds, 1, pl.ds(1, 3))):
        for b in (1, 2):
            for p in range(3):
                to = device(*chip(p, 0, 3 - 2 * b, 0), c)
                n = 4 * p + 2 * (b - 1) + m
                copies.append(remote(meta.at[p, 0, span], meta.at[p, b, span], m2s.at[n], m2r.at[n], to))
                copies.append(remote(tk[p].at[0, span], tk[p].at[b, span], s2s.at[n], s2r.at[n], to))
    for copy in firsts + seconds:
        copy.start()

    slot = lax.broadcasted_iota(jnp.int32, (16, 128), 0).astype(F32)

    def stage(p, b):
        behind = 3 - 2 * b
        groups = [[(chip(p, 0, 0, g), k) for g in range(4) for k in range(2)]]
        if b:
            groups.append([(chip(p, 0, behind, g), b - 1) for g in range(4)])

        def step(a, carry):
            ids, place, gate = meta[p, b, a, 0:8, :], meta[p, b, a, 8:16, :], meta[p, b, a, 16:24, :]
            source = tk[p][b, a]
            for far_off, group in enumerate(groups):
                picks, weights = [], []
                for where, k in group:
                    mine = ids == (expert(*where) + k).astype(F32)
                    at = jnp.sum(jnp.where(mine, place + 1.0, 0.0), axis=0, keepdims=True) - 1.0
                    weight = jnp.sum(jnp.where(mine, gate, 0.0), axis=0, keepdims=True)
                    hit = at == slot
                    picks.append(jnp.where(hit, 1.0, 0.0))
                    weights.append(jnp.where(hit, weight, 0.0))
                chosen = jnp.concatenate(picks, axis=0).astype(BF16)
                weighted = jnp.concatenate(weights, axis=0).astype(BF16)
                block = jnp.dot(chosen, source, preferred_element_type=F32).astype(BF16)
                if far_off:
                    far[p, b - 1, a] = weighted
                    st[p][20 + 4 * b : 24 + 4 * b, a] = block.reshape(4, 16, W[p])
                else:
                    line[p, b, a] = weighted
                    st[p][8 * b : 8 * b + 8, a] = block.reshape(8, 16, W[p])
            return carry

        lax.fori_loop(0, 4, step, 0)

    def columns(half, p):
        return pl.ds(pl.multiple_of(half * HALF + OFF[p], 128), W[p])

    def exchange(q, back, kinds):
        dx = PLACE[q]
        sends = bsem if back else dsem

        def message(p, kind, g, k):
            b, place_b, base = KINDS[kind]
            distant = kind > 2
            behind = (3 - 2 * b) if distant else 0
            place_c = q if p == 1 else g % 2 * 2 + g // 2
            span = q if p == 0 else pl.ds(0, 4)
            cols = columns(k if back else c, p)
            if p == 0:
                there = rows.at[span, place_b, place_c, :, cols]
            elif p == 1:
                there = rows.at[place_c, span, place_b, :, cols]
            else:
                there = rows.at[place_b, place_c, span, :, cols]
            box = ret[p] if back else st[p]
            number = base + g if distant else base + g * 2 + (c if back else k)
            box = box.at[number, span]
            turn = -1 if back else 1
            to = device(*chip(p, 0, turn * behind, turn * g), k)
            src, dst = (there, box) if back else (box, there)
            arrived = rsem.at[p, int(kind == 0)] if back else xsem.at[q]
            if distant:
                remote(src, dst, sends.at[p], arrived, to).start()
                return
            here = jnp.logical_and(g == 0, k == c)

            @pl.when(here)
            def _():
                pltpu.make_async_copy(src, dst, arrived).start()

            @pl.when(jnp.logical_not(here))
            def _():
                remote(src, dst, sends.at[p], arrived, to).start()

        def step(i, carry):
            g = (sign * i + 4) % 4

            def lines(kind, ks):
                for p in (0, 2):
                    if p == 0 or KINDS[kind][1] == q:
                        for k in ks:
                            message(p, kind, g, k)

            for kind in kinds:
                only = KINDS[kind][0] - 1
                if kind < 3:
                    lines(kind, (0, 1))

                    @pl.when(i % 2 == 0)
                    def _():
                        message(1, kind, dx, i // 2)
                elif back:
                    @pl.when(c == only)
                    def _():
                        lines(kind, (0, 1))

                        @pl.when(i % 2 == 0)
                        def _():
                            message(1, kind, dx, i // 2)
                else:
                    lines(kind, (only,))

                    @pl.when(i == 0)
                    def _():
                        message(1, kind, dx, only)
            return carry

        lax.fori_loop(0, 4, step, 0)

    for copy in firsts:
        copy.wait_recv()
    for copy in thirds:
        copy.start()
    for p in range(3):
        stage(p, 0)
    for q in range(4):
        exchange(q, False, (0,))
    for copy in seconds + thirds:
        copy.wait_recv()
    for b in (1, 2):
        for p in range(3):
            stage(p, b)
    for q in range(4):
        exchange(q, False, (1, 2, 3, 4))

    for copy in weights:
        copy.wait()
    for q in range(4):
        await_bytes(rows.at[q], xsem.at[q])

        def up(n, carry):
            cols = pl.ds(pl.multiple_of(n * 256, 256), 256)
            batch = rows[q].reshape(256, D)
            gate = jnp.dot(batch, wg[:, cols], preferred_element_type=F32)
            lift = jnp.dot(batch, wu[:, cols], preferred_element_type=F32)
            hid[:, cols] = (gate / (1.0 + jnp.exp(-gate)) * lift).astype(BF16)
            return carry

        lax.fori_loop(0, FF // 256, up, 0)

        def down(n, carry):
            cols = pl.ds(pl.multiple_of(n * 512, 512), 512)
            answer = jnp.dot(hid[...], wd[:, cols], preferred_element_type=F32).astype(BF16)
            rows[q, :, :, :, cols] = answer.reshape(4, 4, 16, 512)
            return carry

        lax.fori_loop(0, D // 512, down, 0)
        exchange(q, True, (1, 2, 3, 4) if q >= NOW else (0, 1, 2, 3, 4))
    for q in range(NOW, 4):
        exchange(q, True, (0,))

    for copy in firsts + seconds + thirds:
        copy.wait_send()

    def weigh(weighted, answers):
        return lax.dot_general(weighted, answers, (((0,), (0,)), ((), ())), preferred_element_type=F32)

    homeward = []
    for p in range(3):
        await_bytes(ret[p].at[pl.ds(8, 24)], rsem.at[p, 0])
        for b in (1, 2):
            def step(a, carry):
                near = weigh(line[p, b, a], ret[p][8 * b : 8 * b + 8, a].reshape(128, W[p]))
                away = weigh(far[p, b - 1, a], ret[p][20 + 4 * b : 24 + 4 * b, a].reshape(64, W[p]))
                tk[p][b, a] = (near + away).astype(BF16)
                return carry

            lax.fori_loop(0, 4, step, 0)
            n = 2 * p + b - 1
            to = device(*chip(p, 0, 2 * b - 3, 0), c)
            copy = remote(tk[p].at[b], rb[p].at[b - 1], qs.at[n], qr.at[n], to)
            copy.start()
            homeward.append(copy)
    lasts = []
    for p in range(3):
        await_bytes(ret[p].at[pl.ds(0, 8)], rsem.at[p, 1])
        for copy in homeward[2 * p : 2 * p + 2]:
            copy.wait_recv()
        for d in (2, 1, 3, 0):
            a = PLACE[d]
            total = weigh(line[p, 0, a], ret[p][0:8, a].reshape(128, W[p]))
            total = total + (rb[p][0, a].astype(F32) + rb[p][1, a].astype(F32))
            if d == 0:
                tot[:, OFF[p] : OFF[p] + W[p]] = total
            else:
                tk[p][0, a] = total.astype(BF16)
                n = 3 * p + d - 1
                to = device(*chip(p, -d, 0, 0), c)
                copy = remote(tk[p].at[0, a], rs[p].at[a - 1], ps.at[n], pr.at[n], to)
                copy.start()
                lasts.append(copy)
    for copy in lasts:
        copy.wait_recv()
    for p in range(3):
        cols = slice(OFF[p], OFF[p] + W[p])
        tot[:, cols] = tot[:, cols] + (
            rs[p][0].astype(F32) + rs[p][1].astype(F32) + rs[p][2].astype(F32)
        )
    last = remote(tot.at[other_rows], sib, sibs.at[2], sibr.at[2], sibling)
    last.start()
    out_ref[:, own_cols] = (tok_ref[:, own_cols].astype(F32) + tot[own_rows, :]).astype(BF16)
    last.wait_recv()
    out_ref[:, other_cols] = (tok_ref[:, other_cols].astype(F32) + sib[...]).astype(BF16)

    last.wait_send()
    for copy in homeward + lasts:
        copy.wait_send()
    for sems, boxes in ((dsem, st), (bsem, ret)):
        for p in range(3):
            await_bytes(boxes[p].at[pl.ds(0, 29)], sems.at[p])


def shards(tokens, norm_gain, w_gate, w_up, w_down, expert_ids, gate_weights, capacity):
    vmem, dma = pltpu.VMEM, pltpu.SemaphoreType.DMA
    whole = pl.BlockSpec(memory_space=pltpu.VMEM)
    hbm = pl.BlockSpec(memory_space=pl.ANY)
    relay = [vmem((32, 4, 16, w), BF16) for w in W]
    return pl.pallas_call(
        kernel,
        out_shape=jax.ShapeDtypeStruct(tokens.shape, BF16),
        in_specs=[whole, whole, hbm, hbm, hbm, whole, whole, whole],
        out_specs=whole,
        scratch_shapes=[
            vmem((D, FF), BF16), vmem((D, FF), BF16), vmem((FF, D), BF16),
            vmem((64, D), BF16), vmem((128, HALF), BF16),
            vmem((24, 128), F32), vmem((24, 128), F32), vmem((3, 3, 4, 24, 128), F32),
            *[vmem((3, 4, 128, w), BF16) for w in W],
            *relay,
            vmem((4, 4, 4, 16, D), BF16), vmem((256, FF), BF16),
            *relay,
            vmem((3, 3, 4, 128, 128), BF16), vmem((3, 2, 4, 64, 128), BF16),
            *[vmem((2, 4, 128, w), BF16) for w in W],
            *[vmem((3, 128, w), BF16) for w in W],
            vmem((128, HALF), F32), vmem((64, HALF), F32),
            dma((3,)), dma((3,)), dma((3,)), dma((9,)), dma((9,)), dma((9,)), dma((9,)),
            dma((12,)), dma((12,)), dma((12,)), dma((12,)),
            dma((3,)), dma((4,)), dma((3,)), dma((3, 2)), dma((6,)), dma((6,)), dma((9,)), dma((9,)),
        ],
        compiler_params=pltpu.CompilerParams(
            collective_id=0, has_side_effects=True, vmem_limit_bytes=64 * 2**20
        ),
        cost_estimate=pl.CostEstimate(flops=23 * 10**9, bytes_accessed=23 * 10**6, transcendentals=10**6),
    )(
        tokens, norm_gain, w_gate, w_up, w_down, expert_ids.T, gate_weights.T,
        capacity.reshape(1, 128),
    )


def solution(mesh):
    both = ("node", "local")
    in_specs = (
        P(both, None), P(), P(both, None, None), P(both, None, None), P(both, None, None),
        P(both, None), P(both, None), P(),
    )
    return jax.shard_map(shards, mesh=mesh, in_specs=in_specs, out_specs=P(both, None), check_vma=False)
```

```python
import functools

import jax
import jax.numpy as jnp
from jax import lax
from jax.experimental import pallas as pl
from jax.experimental.pallas import tpu as pltpu
from jax.sharding import PartitionSpec as P

MESH = pl.DeviceIdType.MESH
F32, BF16 = jnp.float32, jnp.bfloat16

D = 3584
FF = 1024
HALF = D // 2
W = (640, 640, 512)
OFF = (0, 640, 1280)
AXES = ((0, 1, 2), (1, 2, 0), (2, 0, 1))
NOW = 4
PLACE = (0, 2, 1, 3)
KINDS = ((0, 0, 0), (1, 2, 8), (2, 3, 16), (1, 1, 24), (2, 1, 28))


def device(x, y, z, c):
    return (y * 4 + z, x * 2 + c)


def expert(x, y, z):
    return (y * 4 + z) * 8 + x * 2


def kernel(
    tok_ref, gain_ref, wg_hbm, wu_hbm, wd_hbm, ids_ref, gates_ref, cap_ref, out_ref,
    wg, wu, wd, normed, tokh, own_info, sib_info, meta, tk0, tk1, tk2,
    st0, st1, st2, rows, hid, ret0, ret1, ret2, line, far,
    rb0, rb1, rb2, rs0, rs1, rs2, tot, sib,
    wsem, sibs, sibr, s1s, s1r, mts, mtr, s2s, s2r, m2s, m2r, dsem, xsem, bsem, rsem, qs, qr, ps, pr,
):
    node, local = lax.axis_index("node"), lax.axis_index("local")
    x, y, z, c = local // 2, node // 4, node % 4, local % 2
    sign = 1 - 2 * c
    tk, st, ret, rb, rs = (tk0, tk1, tk2), (st0, st1, st2), (ret0, ret1, ret2), (rb0, rb1, rb2), (rs0, rs1, rs2)

    def moved(t, da, db, dc):
        place = [x, y, z]
        for axis, d in zip(AXES[t], (da, db, dc)):
            place[axis] = (place[axis] + d + 4) % 4
        return place

    def chip(p, da, db, dc):
        if p == 0:
            return moved(0, da, db, dc)
        return [jnp.where(c == 0, u, v) for u, v in zip(moved(p, da, db, dc), moved(3 - p, da, db, dc))]

    def remote(src, dst, send, recv, to):
        return pltpu.make_async_remote_copy(
            src_ref=src, dst_ref=dst, send_sem=send, recv_sem=recv, device_id=to, device_id_type=MESH
        )

    def await_bytes(ref, sem):
        pltpu.make_async_copy(ref, ref, sem).wait()

    weights = [
        pltpu.make_async_copy(w_hbm.at[0], w_vmem, wsem.at[i])
        for i, (w_hbm, w_vmem) in enumerate(((wg_hbm, wg), (wu_hbm, wu), (wd_hbm, wd)))
    ]

    barrier = pltpu.get_barrier_semaphore()
    partners = 0
    for dx in range(4):
        for dy in range(4):
            for dz in range(4):
                if dx and dy and dz or (dx, dy) == (0, 2) and dz or (dy, dz) == (0, 2) and dx or (dz, dx) == (0, 2) and dy:
                    continue
                for k in range(2):
                    if dx == dy == dz == 0 and k == 0:
                        continue
                    partners += 1
                    pl.semaphore_signal(
                        barrier, inc=1, device_id_type=MESH,
                        device_id=device((x + dx) % 4, (y + dy) % 4, (z + dz) % 4, (c + k) % 2),
                    )

    resid = tok_ref[...].astype(F32)
    scale = lax.rsqrt(jnp.mean(resid * resid, axis=-1, keepdims=True) + 1e-06)
    normed[...] = (resid * scale * gain_ref[...].reshape(1, D)).astype(BF16)
    for copy in weights:
        copy.start()

    twice = lambda a: jnp.concatenate([a, a], axis=1)
    ids = twice(ids_ref[...])
    names = lax.broadcasted_iota(jnp.int32, (128, 128), 0)
    lanes = lax.broadcasted_iota(jnp.int32, (128, 128), 1)
    hits = [ids[k : k + 1, :] == names for k in range(8)]
    named = functools.reduce(jnp.logical_or, hits)
    earlier = jnp.logical_and(names < lanes, names // 32 == lanes // 32)
    before = jnp.dot(
        named.astype(F32).astype(BF16), earlier.astype(F32).astype(BF16), preferred_element_type=F32
    )
    group = (lanes // 32 % 2 + c * 2).astype(F32)
    limit = jnp.transpose(jnp.broadcast_to(cap_ref[...].astype(F32), (128, 128)))
    place = jnp.where(before < limit, group * 4.0 + before, -1.0)
    own_info[0:8, :] = ids.astype(F32)
    for k in range(8):
        own_info[8 + k : 9 + k, :] = jnp.sum(jnp.where(hits[k], place, 0.0), axis=0, keepdims=True)
    own_info[16:24, :] = twice(gates_ref[...])
    own_rows = pl.ds(pl.multiple_of(c * 64, 64), 64)
    other_rows = pl.ds(pl.multiple_of((1 - c) * 64, 64), 64)
    own_cols = pl.ds(pl.multiple_of(c * HALF, 128), HALF)
    other_cols = pl.ds(pl.multiple_of((1 - c) * HALF, 128), HALF)
    tokh[own_rows, :] = normed[:, own_cols]

    pl.semaphore_wait(barrier, partners)

    sibling = device(x, y, z, 1 - c)
    swap = (
        remote(normed.at[:, other_cols], tokh.at[own_rows], sibs.at[0], sibr.at[0], sibling),
        remote(own_info, sib_info, sibs.at[1], sibr.at[1], sibling),
    )
    for copy in swap:
        copy.start()
    for copy in swap:
        copy.wait()
    side = lax.broadcasted_iota(jnp.int32, (24, 128), 1) // 64
    for p in range(3):
        meta[p, 0, 0] = jnp.where(side == c, own_info[...], sib_info[...])
        tk[p][0, 0] = tokh[:, OFF[p] : OFF[p] + W[p]]

    firsts, seconds, thirds = [], [], []
    for d in (1, 3, 2):
        for p in range(3):
            to = device(*chip(p, d, 0, 0), c)
            n = 3 * p + d - 1
            firsts.append(remote(meta.at[p, 0, 0], meta.at[p, 0, PLACE[d]], mts.at[n], mtr.at[n], to))
            firsts.append(remote(tk[p].at[0, 0], tk[p].at[0, PLACE[d]], s1s.at[n], s1r.at[n], to))
    for copies, m, span in ((seconds, 0, pl.ds(0, 1)), (thirds, 1, pl.ds(1, 3))):
        for b in (1, 2):
            for p in range(3):
                to = device(*chip(p, 0, 3 - 2 * b, 0), c)
                n = 4 * p + 2 * (b - 1) + m
                copies.append(remote(meta.at[p, 0, span], meta.at[p, b, span], m2s.at[n], m2r.at[n], to))
                copies.append(remote(tk[p].at[0, span], tk[p].at[b, span], s2s.at[n], s2r.at[n], to))
    for copy in firsts + seconds:
        copy.start()

    slot = lax.broadcasted_iota(jnp.int32, (16, 128), 0).astype(F32)

    def stage(p, b):
        behind = 3 - 2 * b
        groups = [[(chip(p, 0, 0, g), k) for g in range(4) for k in range(2)]]
        if b:
            groups.append([(chip(p, 0, behind, g), b - 1) for g in range(4)])

        def step(a, carry):
            ids, place, gate = meta[p, b, a, 0:8, :], meta[p, b, a, 8:16, :], meta[p, b, a, 16:24, :]
            source = tk[p][b, a]
            for far_off, group in enumerate(groups):
                picks, weights = [], []
                for where, k in group:
                    mine = ids == (expert(*where) + k).astype(F32)
                    at = jnp.sum(jnp.where(mine, place + 1.0, 0.0), axis=0, keepdims=True) - 1.0
                    weight = jnp.sum(jnp.where(mine, gate, 0.0), axis=0, keepdims=True)
                    hit = at == slot
                    picks.append(jnp.where(hit, 1.0, 0.0))
                    weights.append(jnp.where(hit, weight, 0.0))
                chosen = jnp.concatenate(picks, axis=0).astype(BF16)
                weighted = jnp.concatenate(weights, axis=0).astype(BF16)
                block = jnp.dot(chosen, source, preferred_element_type=F32).astype(BF16)
                if far_off:
                    far[p, b - 1, a] = weighted
                    st[p][20 + 4 * b : 24 + 4 * b, a] = block.reshape(4, 16, W[p])
                else:
                    line[p, b, a] = jnp.transpose(jnp.concatenate(weights, axis=0)).astype(BF16)
                    st[p][8 * b : 8 * b + 8, a] = block.reshape(8, 16, W[p])
            return carry

        lax.fori_loop(0, 4, step, 0)

    def columns(half, p):
        return pl.ds(pl.multiple_of(half * HALF + OFF[p], 128), W[p])

    def exchange(q, back, kinds):
        dx = PLACE[q]
        sends = bsem if back else dsem

        def message(t, r, kind, g, k):
            p = 3 - t if t and r else t
            b, place_b, base = KINDS[kind]
            distant = kind > 2
            behind = (3 - 2 * b) if distant else 0
            place_c = q if t == 1 else g % 2 * 2 + g // 2
            span = q if t == 0 else pl.ds(0, 4)
            cols = columns(r, p)
            if t == 0:
                there = rows.at[span, place_b, place_c, :, cols]
            elif t == 1:
                there = rows.at[place_c, span, place_b, :, cols]
            else:
                there = rows.at[place_b, place_c, span, :, cols]
            box = ret[p] if back else st[p]
            number = base + g if distant else base + g * 2 + (c if back else k)
            box = box.at[number, span]
            turn = -1 if back else 1
            to = device(*moved(t, 0, turn * behind, turn * g), r if back else k)
            src, dst = (there, box) if back else (box, there)
            arrived = rsem.at[p, int(kind == 0)] if back else xsem.at[q]
            if distant:
                remote(src, dst, sends.at[p], arrived, to).start()
                return
            here = jnp.logical_and(g == 0, c == (r if back else k))

            @pl.when(here)
            def _():
                pltpu.make_async_copy(src, dst, arrived).start()

            @pl.when(jnp.logical_not(here))
            def _():
                remote(src, dst, sends.at[p], arrived, to).start()

        def step(i, carry):
            g = (sign * i + 4) % 4

            def batch(kind, pairs):
                for t in (0, 2):
                    if t == 0 or KINDS[kind][1] == q:
                        for r, k in pairs:
                            message(t, r, kind, g, k)
                for r, k in pairs:
                    @pl.when(i == 2 * (r if back else k))
                    def _():
                        message(1, r, kind, dx, k)

            for kind in kinds:
                only = KINDS[kind][0] - 1
                if back and kind < 3:
                    batch(kind, ((0, None), (1, None)))
                elif back:
                    @pl.when(c == only)
                    def _():
                        batch(kind, ((0, None), (1, None)))
                else:
                    for r in range(2):
                        @pl.when(c == r)
                        def _():
                            batch(kind, ((r, 0), (r, 1)) if kind < 3 else ((r, only),))
            return carry

        lax.fori_loop(0, 4, step, 0)

    for copy in firsts:
        copy.wait_recv()
    for copy in thirds:
        copy.start()
    for p in range(3):
        stage(p, 0)
    for q in range(4):
        exchange(q, False, (0,))
    for copy in seconds + thirds:
        copy.wait_recv()
    for b in (1, 2):
        for p in range(3):
            stage(p, b)
    for q in range(4):
        exchange(q, False, (1, 2, 3, 4))

    for copy in weights:
        copy.wait()
    for q in range(4):
        await_bytes(rows.at[q], xsem.at[q])

        def up(n, carry):
            cols = pl.ds(pl.multiple_of(n * 256, 256), 256)
            batch = rows[q].reshape(256, D)
            gate = jnp.dot(batch, wg[:, cols], preferred_element_type=F32)
            lift = jnp.dot(batch, wu[:, cols], preferred_element_type=F32)
            hid[:, cols] = (gate / (1.0 + jnp.exp(-gate)) * lift).astype(BF16)
            return carry

        lax.fori_loop(0, FF // 256, up, 0)

        def down(n, carry):
            cols = pl.ds(pl.multiple_of(n * 512, 512), 512)
            answer = jnp.dot(hid[...], wd[:, cols], preferred_element_type=F32).astype(BF16)
            rows[q, :, :, :, cols] = answer.reshape(4, 4, 16, 512)
            return carry

        lax.fori_loop(0, D // 512, down, 0)
        exchange(q, True, (1, 2, 3, 4, 0))
    for q in range(NOW, 4):
        exchange(q, True, (0,))

    for copy in firsts + seconds + thirds:
        copy.wait_send()

    def weigh(weighted, answers):
        return lax.dot_general(weighted, answers, (((0,), (0,)), ((), ())), preferred_element_type=F32)

    homeward = []
    for p in range(3):
        await_bytes(ret[p].at[pl.ds(8, 24)], rsem.at[p, 0])
        for b in (1, 2):
            def step(a, carry):
                near = jnp.dot(line[p, b, a], ret[p][8 * b : 8 * b + 8, a].reshape(128, W[p]), preferred_element_type=F32)
                away = weigh(far[p, b - 1, a], ret[p][20 + 4 * b : 24 + 4 * b, a].reshape(64, W[p]))
                tk[p][b, a] = (near + away).astype(BF16)
                return carry

            lax.fori_loop(0, 4, step, 0)
            n = 2 * p + b - 1
            to = device(*chip(p, 0, 2 * b - 3, 0), c)
            copy = remote(tk[p].at[b], rb[p].at[b - 1], qs.at[n], qr.at[n], to)
            copy.start()
            homeward.append(copy)
    lasts = []
    for p in range(3):
        await_bytes(ret[p].at[pl.ds(0, 8)], rsem.at[p, 1])
        for copy in homeward[2 * p : 2 * p + 2]:
            copy.wait_recv()
        for d in (2, 1, 3, 0):
            a = PLACE[d]
            total = jnp.dot(line[p, 0, a], ret[p][0:8, a].reshape(128, W[p]), preferred_element_type=F32)
            total = total + (rb[p][0, a].astype(F32) + rb[p][1, a].astype(F32))
            if d == 0:
                tot[:, OFF[p] : OFF[p] + W[p]] = total
            else:
                tk[p][0, a] = total.astype(BF16)
                n = 3 * p + d - 1
                to = device(*chip(p, -d, 0, 0), c)
                copy = remote(tk[p].at[0, a], rs[p].at[a - 1], ps.at[n], pr.at[n], to)
                copy.start()
                lasts.append(copy)
    for copy in lasts:
        copy.wait_recv()
    for p in range(3):
        cols = slice(OFF[p], OFF[p] + W[p])
        tot[:, cols] = tot[:, cols] + (
            rs[p][0].astype(F32) + rs[p][1].astype(F32) + rs[p][2].astype(F32)
        )
    last = remote(tot.at[other_rows], sib, sibs.at[2], sibr.at[2], sibling)
    last.start()
    out_ref[:, own_cols] = (tok_ref[:, own_cols].astype(F32) + tot[own_rows, :]).astype(BF16)
    last.wait_recv()
    out_ref[:, other_cols] = (tok_ref[:, other_cols].astype(F32) + sib[...]).astype(BF16)

    last.wait_send()
    for copy in homeward + lasts:
        copy.wait_send()
    for sems, boxes in ((dsem, st), (bsem, ret)):
        for p in range(3):
            await_bytes(boxes[p].at[pl.ds(0, 29)], sems.at[p])


def shards(tokens, norm_gain, w_gate, w_up, w_down, expert_ids, gate_weights, capacity):
    vmem, dma = pltpu.VMEM, pltpu.SemaphoreType.DMA
    whole = pl.BlockSpec(memory_space=pltpu.VMEM)
    hbm = pl.BlockSpec(memory_space=pl.ANY)
    relay = [vmem((32, 4, 16, w), BF16) for w in W]
    return pl.pallas_call(
        kernel,
        out_shape=jax.ShapeDtypeStruct(tokens.shape, BF16),
        in_specs=[whole, whole, hbm, hbm, hbm, whole, whole, whole],
        out_specs=whole,
        scratch_shapes=[
            vmem((D, FF), BF16), vmem((D, FF), BF16), vmem((FF, D), BF16),
            vmem((64, D), BF16), vmem((128, HALF), BF16),
            vmem((24, 128), F32), vmem((24, 128), F32), vmem((3, 3, 4, 24, 128), F32),
            *[vmem((3, 4, 128, w), BF16) for w in W],
            *relay,
            vmem((4, 4, 4, 16, D), BF16), vmem((256, FF), BF16),
            *relay,
            vmem((3, 3, 4, 128, 128), BF16), vmem((3, 2, 4, 64, 128), BF16),
            *[vmem((2, 4, 128, w), BF16) for w in W],
            *[vmem((3, 128, w), BF16) for w in W],
            vmem((128, HALF), F32), vmem((64, HALF), F32),
            dma((3,)), dma((3,)), dma((3,)), dma((9,)), dma((9,)), dma((9,)), dma((9,)),
            dma((12,)), dma((12,)), dma((12,)), dma((12,)),
            dma((3,)), dma((4,)), dma((3,)), dma((3, 2)), dma((6,)), dma((6,)), dma((9,)), dma((9,)),
        ],
        compiler_params=pltpu.CompilerParams(
            collective_id=0, has_side_effects=True, vmem_limit_bytes=64 * 2**20
        ),
        cost_estimate=pl.CostEstimate(flops=23 * 10**9, bytes_accessed=23 * 10**6, transcendentals=10**6),
    )(
        tokens, norm_gain, w_gate, w_up, w_down, expert_ids.T, gate_weights.T,
        capacity.reshape(1, 128),
    )


def solution(mesh):
    both = ("node", "local")
    in_specs = (
        P(both, None), P(), P(both, None, None), P(both, None, None), P(both, None, None),
        P(both, None), P(both, None), P(),
    )
    return jax.shard_map(shards, mesh=mesh, in_specs=in_specs, out_specs=P(both, None), check_vma=False)
```
